512 devices in a mesh: in: 8 (over x, z_lo), out: 8 (over z_hi, core), batch: 8 (over y).
Axes of the slice: x: 4, y: 8, z: 8 (z_hi: 4, z_lo: 2; z = z_hi * 2 + z_lo), core: 2. Of those that a mesh axis runs over, the one named last changes fastest.
Arguments:
- inputs: bfloat16 [2048, 6144], P('batch', 'in'), may hold values from -6 to 6
- out_grad: bfloat16 [2048, 6144], P('batch', 'in'), may hold values from -6 to 6
- pre_act: bfloat16 [2048, 8192], P('batch', 'out'), may hold values from -6 to 6
- w_in: bfloat16 [6144, 8192], P('in', 'out'), may hold values from -0.078125 to 0.078125
- w_out: bfloat16 [8192, 6144], P('out', 'in'), may hold values from -0.0625 to 0.0625
Outputs:
- input_grad: bfloat16 [2048, 6144], P('batch', ('in', 'out'))
- w_in_grad: bfloat16 [6144, 8192], P('in', ('out', 'batch'))
- w_out_grad: bfloat16 [8192, 6144], P('out', ('in', 'batch'))
The draws below stay inside these ranges and needn't reach their ends.
All inputs are finite; a program needn't handle non-finite values.
Results may differ from the reference program's by a relative error of at most 0.025.
Values may be sent and summed in bfloat16 or wider, within the bound.
No kernel may reach another device: no remote copies, remote signals or barrier semaphores. Data moves between devices by JAX's collectives and lax.ppermute only.
A program may use at most 64 MiB of HBM per device.

```python
import math
import jax
import jax.numpy as jnp
from jax import lax

D = 6144
FF = 8192
TOK_DEV = 256
TOKENS = 2048
N_IN = 8
N_OUT = 8
N_BATCH = 8


def raised(array, own_key, source, target, blocks, factor):
    owner, partner = [(jnp.arange(array.shape[axis_at]) // (array.shape[axis_at] // blocks)).reshape([-1 if axis == axis_at else 1 for axis in range(array.ndim)]) for axis_at in (source, target)]
    chosen = jax.random.permutation(own_key, blocks)[partner]
    strong = (owner == chosen) | (owner == (partner + blocks // 2) % blocks)
    return jnp.where(strong, factor * array, array)


def level_of(stream_key, shape, split, smallest, top_value):
    factor_of, own = 1.0, jax.random.fold_in(stream_key, 6)
    for axis_at, parts in split:
        heights = jnp.exp(jax.random.uniform(jax.random.fold_in(own, axis_at), (parts,), jnp.float32, smallest / len(split), top_value / len(split)))
        factor_of = factor_of * jnp.repeat(heights, shape[axis_at] // parts).reshape([-1 if axis == axis_at else 1 for axis in range(len(shape))])
    return factor_of


def bell_draw(rng, extent, scale, limit, pieces=(), dtype=jnp.bfloat16):
    factor_of = level_of(rng, extent, pieces, -0.22, 0.18) if pieces else 1.0
    entries = jax.random.normal(rng, extent, jnp.float32) * scale * factor_of
    return jnp.minimum(jnp.maximum(entries, -limit), limit).astype(dtype)


def bell_draw_with(own_key, dims, scale, reach, pieces, heavy, dtype=jnp.bfloat16):
    entries = scale * jax.random.normal(own_key, dims, jnp.float32)
    if pieces:
        entries = entries * level_of(own_key, dims, pieces, -0.22, 0.18)
    return jnp.clip(raised(entries, jax.random.fold_in(own_key, 3), *heavy), -reach, reach).astype(dtype)


def setup_inputs(seed: int = 0) -> dict:
    keys = jax.random.split(jax.random.key(seed), 6)
    inputs = bell_draw(keys[0], (TOKENS, D), 1.0, 6.0, ((0, 8), (1, 8)))
    out_grad = bell_draw_with(keys[1], (TOKENS, D), 1.0, 6.0, ((0, 8), (1, 8)), (0, 1, 8, 2.0))
    pre_act = bell_draw(keys[2], (TOKENS, FF), 1.5, 6.0, ((0, 8), (1, 8)))
    w_in = bell_draw(keys[3], (D, FF), D ** -0.5, 0.078125, ((0, 8), (1, 8)))
    w_out = bell_draw(keys[4], (FF, D), FF ** -0.5, 0.0625, ((0, 8), (1, 8)))
    return {"inputs": inputs, "out_grad": out_grad, "pre_act": pre_act, "w_in": w_in, "w_out": w_out}


def gelu_parts(pre):
    value = pre.astype(jnp.float32)
    cdf = 0.5 * (1.0 + lax.erf(value * 0.7071067811865476))
    density = jnp.exp(-0.5 * value * value) * 0.3989422804014327
    return (value * cdf, cdf + value * density)

def rounded(part):
    held = lax.optimization_barrier(part.astype(jnp.bfloat16))
    return held.astype(jnp.float32)

def block_sum(left, right, count, width, left_dim, right_dim, contract, shape, factor):

    def one_block(index, total):
        start = (index * width).astype(jnp.int32)
        left_block = lax.dynamic_slice_in_dim(left, start, width, left_dim)
        right_block = lax.dynamic_slice_in_dim(right, start, width, right_dim)
        part = lax.dot_general(left_block, right_block, contract, preferred_element_type=jnp.float32)
        return total + rounded(part * factor)
    return lax.fori_loop(0, count, one_block, jnp.zeros(shape, jnp.float32))

def reference(inputs, out_grad, pre_act, w_in, w_out):
    act_full, deriv = gelu_parts(pre_act)
    act = act_full.astype(jnp.bfloat16)
    act_grad = block_sum(out_grad, w_out, N_IN, D // N_IN, 1, 1, (((1,), (1,)), ((), ())), (TOKENS, FF), 1.0)
    pre_grad = (act_grad * deriv).astype(jnp.bfloat16)
    input_grad = block_sum(pre_grad, w_in, N_OUT, FF // N_OUT, 1, 1, (((1,), (1,)), ((), ())), (TOKENS, D), 1.0)
    factor = 1.0 / math.sqrt(TOKENS)
    w_in_grad = block_sum(inputs, pre_grad, N_BATCH, TOK_DEV, 0, 0, (((0,), (0,)), ((), ())), (D, FF), factor)
    w_out_grad = block_sum(act, out_grad, N_BATCH, TOK_DEV, 0, 0, (((0,), (0,)), ((), ())), (FF, D), factor)
    return (input_grad.astype(jnp.bfloat16), w_in_grad.astype(jnp.bfloat16), w_out_grad.astype(jnp.bfloat16))
```

```python
import math

import jax
import jax.numpy as jnp
from jax import lax
from jax.sharding import Mesh, PartitionSpec as P

BF = jnp.bfloat16
F32 = jnp.float32
IN = ("x", "zlo")
OUT = ("zhi", "core")
SWAP = [(0, 1), (1, 0)]


def cdf_of(value):
    return 0.5 * (1.0 + lax.erf(value * 0.7071067811865476))


def density_of(value):
    return jnp.exp(-0.5 * value * value) * 0.3989422804014327


def nt(a, b):
    return lax.dot_general(a, b, (((1,), (1,)), ((), ())), preferred_element_type=F32)


def tn(a, b):
    return lax.dot_general(a, b, (((0,), (0,)), ((), ())), preferred_element_type=F32)


def per_device(inputs, out_grad, pre_act, w_in, w_out):
    tok, d_in = inputs.shape
    hid = pre_act.shape[1]
    n_in, n_b = 8, 8
    core = lax.axis_index("core")
    y = lax.axis_index("batch")
    i = lax.axis_index(IN)
    factor = 1.0 / math.sqrt(tok * n_b)
    rows = tok // n_in
    ring = [(b, (b + 1) % n_b) for b in range(n_b)] + [
        (n_b + b, n_b + (b - 1) % n_b) for b in range(n_b)
    ]

    part = nt(out_grad, w_out).astype(BF).reshape(n_in, rows, hid)
    got = lax.all_to_all(part, IN, 0, 0, tiled=True)
    act_grad = jnp.sum(got.astype(F32), axis=0)
    v = lax.dynamic_slice_in_dim(pre_act, i * rows, rows, 0).astype(F32)
    deriv = cdf_of(v) + v * density_of(v)
    mine = (act_grad * deriv).astype(BF)
    pre_grad = lax.all_to_all(
        jnp.broadcast_to(mine, (n_in, rows, hid)), IN, 0, 0, tiled=True
    ).reshape(tok, hid)

    x1 = lax.ppermute(inputs, ("core", "batch"), ring)
    x2 = lax.ppermute(x1, ("core", "batch"), ring)
    x3 = lax.ppermute(x2, ("core", "batch"), ring)
    half = lax.dynamic_slice_in_dim(x3, core * (tok // 2), tok // 2, 0)
    x4 = lax.ppermute(half, ("core", "batch"), ring)
    side = jnp.concatenate([x1, x2, x3, x4], 0)
    other = lax.ppermute(side, "core", SWAP)

    pa = pre_act.astype(F32)
    act = (pa * cdf_of(pa)).astype(BF)
    w_out_term = (tn(out_grad, act) * factor).astype(BF)
    w_out_grad = lax.psum_scatter(w_out_term, "batch", scatter_dimension=0, tiled=True).T

    w4 = w_in.reshape(4, 2, d_in // 8, hid)
    w_far = lax.dynamic_index_in_dim(w4, 1 - core, 1, False).reshape(d_in // 2, hid)
    w_near = lax.dynamic_index_in_dim(w4, core, 1, False).reshape(d_in // 2, hid)
    far = nt(w_far, pre_grad).astype(BF)
    near = nt(w_near, pre_grad)
    pair = (near + lax.ppermute(far, "core", SWAP).astype(F32)).astype(BF)
    quad = lax.all_to_all(pair.reshape(4, d_in // 8, tok), "zhi", 0, 0, tiled=True)
    input_grad = jnp.sum(quad.astype(F32), axis=0).astype(BF).T

    cols = pre_grad.reshape(tok, n_b, hid // n_b).swapaxes(0, 1)
    pg = lax.all_to_all(cols, "batch", 0, 0, tiled=True)
    sign = 1 - 2 * core
    take = lambda k: lax.dynamic_index_in_dim(pg, (y + k + n_b) % n_b, 0, False)
    opp = take(4)
    opp_a = lax.dynamic_slice_in_dim(opp, core * (tok // 2), tok // 2, 0)
    opp_b = lax.dynamic_slice_in_dim(opp, (1 - core) * (tok // 2), tok // 2, 0)
    left = jnp.concatenate([inputs, side, other], 0)
    right = jnp.concatenate(
        [pg[y], take(-sign), take(-2 * sign), take(-3 * sign), opp_a]
        + [take(sign), take(2 * sign), take(3 * sign), opp_b],
        0,
    )
    w_in_grad = (tn(left, right) * factor).astype(BF)
    return (input_grad, w_in_grad, w_out_grad)


def solution(mesh):
    fine = Mesh(mesh.devices.reshape(4, 2, 4, 2, 8), ("x", "zlo", "zhi", "core", "batch"))
    return jax.shard_map(
        per_device,
        mesh=fine,
        in_specs=(
            P("batch", IN),
            P("batch", IN),
            P("batch", OUT),
            P(IN, OUT),
            P(OUT, IN),
        ),
        out_specs=(P("batch", IN + OUT), P(IN, OUT + ("batch",)), P(OUT, IN + ("batch",))),
        check_vma=False,
    )
```

```python
import functools
import math

import jax
import jax.numpy as jnp
from jax import lax
from jax.experimental import pallas as pl
from jax.experimental.pallas import tpu as pltpu
from jax.sharding import Mesh, PartitionSpec as P

BF = jnp.bfloat16
F32 = jnp.float32
IN = ("x", "zlo")
OUT = ("zhi", "core")
SWAP = [(0, 1), (1, 0)]
N = 8
RING = [(b, (b + 1) % N) for b in range(N)] + [(N + b, N + (b - 1) % N) for b in range(N)]


def sds(shape, dtype=BF):
    return jax.ShapeDtypeStruct(shape, dtype)


def call(body, outs, *args, any_tail=0, flops=0, touched=0):
    vm = pl.BlockSpec(memory_space=pltpu.VMEM)
    hold = pl.BlockSpec(memory_space=pl.ANY)
    many = isinstance(outs, (list, tuple))
    return pl.pallas_call(
        body,
        out_shape=outs,
        in_specs=[vm] * (len(args) - any_tail) + [hold] * any_tail,
        out_specs=[vm] * len(outs) if many else vm,
        compiler_params=pltpu.CompilerParams(vmem_limit_bytes=40 * 1024 * 1024),
    )(*args)


def cdf_of(value):
    return 0.5 * (1.0 + lax.erf(value * 0.7071067811865476))


def density_of(value):
    return jnp.exp(-0.5 * value * value) * 0.3989422804014327


def dot(a, b):
    return jnp.dot(a, b, preferred_element_type=F32)


def ring_sign():
    return 1 - 2 * lax.axis_index("core")


def own_terms(factor, out_grad, pre, terms, turned, deriv):
    y, s = lax.axis_index("batch"), ring_sign()
    v = pre[...].astype(F32)
    act = (v * cdf_of(v)).astype(BF)
    flipped = out_grad[...].T
    turned[...] = flipped
    width = flipped.shape[0] // N
    for k in range(5):
        at = pl.multiple_of(((y + s * k + N) % N) * width, width)
        terms[k] = (dot(turned[pl.ds(at, width), :], act) * factor).astype(BF)
    i = lax.axis_index(IN)
    wide = pre.shape[1] // N
    u = pre[:, pl.ds(pl.multiple_of(i * wide, wide), wide)].astype(F32)
    deriv[...] = (cdf_of(u) + u * density_of(u)).T


def far_terms(factor, turned, pre, terms):
    y, s = lax.axis_index("batch"), ring_sign()
    v = pre[...].astype(F32)
    act = (v * cdf_of(v)).astype(BF)
    width = turned.shape[0] // N
    for k in range(1, 4):
        at = pl.multiple_of(((y + s * k + N) % N) * width, width)
        terms[k - 1] = (dot(turned[pl.ds(at, width), :], act) * factor).astype(BF)


def hidden_grad(got, deriv, out):
    total = got[0].astype(F32)
    for k in range(1, N):
        total = total + got[k].astype(F32)
    mine = (total * deriv[...]).astype(BF)
    for k in range(N):
        out[k] = mine


def first_add(got, own, far, out):
    out[0] = (got[...].astype(F32) + own[3].astype(F32)).astype(BF)
    out[1] = far[2]


def next_add(k, got, own, far, out):
    out[0] = (got[0].astype(F32) + own[k].astype(F32)).astype(BF)
    out[1] = (got[1].astype(F32) + far[k - 1].astype(F32)).astype(BF)


def last_add(got, other, own, out):
    out[...] = (got[0].astype(F32) + other[...].astype(F32) + own[0].astype(F32)).astype(BF)


def send_half(w, pg, out):
    c = lax.axis_index("core")
    width = w.shape[0] // N
    for z in range(4):
        at = pl.multiple_of((2 * z + 1 - c) * width, width)
        out[z] = dot(w[pl.ds(at, width), :], pg[...]).astype(BF)


def keep_half(w, pg, got, *outs):
    c, zhi = lax.axis_index("core"), lax.axis_index("zhi")
    width = w.shape[0] // N
    for s in range(4):
        z = (zhi + s) % 4
        at = pl.multiple_of((2 * z + c) * width, width)
        outs[s][...] = (dot(w[pl.ds(at, width), :], pg[...]) + got[z].astype(F32)).astype(BF)


def sum_four(a, b, c, d, out):
    total = a[...].astype(F32) + b[...].astype(F32) + c[...].astype(F32) + d[...].astype(F32)
    out[...] = total.astype(BF)


def weight_grad(factor, pg, x0, x1, x2, x3, x4, z1, z2, z3, out):
    y, s = lax.axis_index("batch"), ring_sign()
    total = dot(pg[y], x0[...])
    for k, ref in ((-1, x1), (-2, x2), (-3, x3), (4, x4), (1, z1), (2, z2), (3, z3)):
        total = total + dot(pg[(y + s * k + N) % N], ref[...])
    out[...] = (total * factor).T.astype(BF)


def per_device(inputs, out_grad, pre_act, w_in, w_out):
    tok, d_in = inputs.shape
    hid = pre_act.shape[1]
    factor = 1.0 / math.sqrt(tok * N)
    piece, wide = d_in // N, hid // N
    up = lambda a: lax.ppermute(a, ("core", "batch"), RING)
    swap = lambda a: lax.ppermute(a, "core", SWAP)

    x1 = up(inputs)
    pre_far = swap(pre_act)

    part = lax.dot_general(w_out, out_grad, (((1,), (1,)), ((), ())), preferred_element_type=F32)
    got = lax.all_to_all(part.astype(BF).reshape(N, wide, tok), IN, 0, 0, tiled=True)

    own, turned, deriv = call(
        functools.partial(own_terms, factor),
        [sds((5, piece, hid)), sds((d_in, tok)), sds((wide, tok), F32)],
        out_grad,
        pre_act,
    )
    far = call(functools.partial(far_terms, factor), sds((3, piece, hid)), turned, pre_far)
    x2 = up(x1)

    spread = call(hidden_grad, sds((N, wide, tok)), got, deriv)
    pg = lax.all_to_all(spread, IN, 0, 0, tiled=True)

    r1 = up(own[4])
    t2 = call(first_add, sds((2, piece, hid)), r1, own, far)
    x3 = up(x2)

    cols = lax.all_to_all(pg, "batch", 0, 0, tiled=True)
    pg_flat = pg.reshape(hid, tok)
    far_half = call(send_half, sds((4, piece, tok)), w_in, pg_flat)
    kept = call(keep_half, [sds((piece, tok))] * 4, w_in, pg_flat, swap(far_half))
    parts = [kept[0]] + [
        lax.ppermute(kept[s], "zhi", [(z, (z + s) % 4) for z in range(4)]) for s in range(1, 4)
    ]
    input_grad = call(sum_four, sds((piece, tok)), *parts).T

    r2 = up(t2)
    t3 = call(functools.partial(next_add, 2), sds((2, piece, hid)), r2, own, far)
    x4 = up(x3)
    r3 = up(t3)
    t4 = call(functools.partial(next_add, 1), sds((2, piece, hid)), r3, own, far)
    r4 = up(t4)
    w_out_grad = call(last_add, sds((piece, hid)), r4, swap(r4[1]), own).T

    w_in_grad = call(
        functools.partial(weight_grad, factor),
        sds((d_in, wide)),
        cols, inputs, x1, x2, x3, x4, swap(x1), swap(x2), swap(x3),
    )
    return (input_grad, w_in_grad, w_out_grad)


def solution(mesh):
    fine = Mesh(mesh.devices.reshape(4, 2, 4, 2, 8), ("x", "zlo", "zhi", "core", "batch"))
    return jax.shard_map(
        per_device,
        mesh=fine,
        in_specs=(P("batch", IN), P("batch", IN), P("batch", OUT), P(IN, OUT), P(OUT, IN)),
        out_specs=(P("batch", IN + OUT), P(IN, OUT + ("batch",)), P(OUT, IN + ("batch",))),
        check_vma=False,
    )
```

```python
import functools
import math

import jax
import jax.numpy as jnp
from jax import lax
from jax.experimental import pallas as pl
from jax.experimental.pallas import tpu as pltpu
from jax.sharding import Mesh, PartitionSpec as P

BF = jnp.bfloat16
F32 = jnp.float32
IN = ("x", "zlo")
OUT = ("zhi", "core")
SWAP = [(0, 1), (1, 0)]
N = 8


def sds(shape, dtype=BF):
    return jax.ShapeDtypeStruct(shape, dtype)


def call(body, outs, *args, scratch=(), flops=0, touched=0, hold=0):
    vm = pl.BlockSpec(memory_space=pltpu.VMEM)
    many = isinstance(outs, (list, tuple))
    return pl.pallas_call(
        body,
        out_shape=outs,
        in_specs=[vm] * (len(args) - hold) + [pl.BlockSpec(memory_space=pl.ANY)] * hold,
        out_specs=[vm] * len(outs) if many else vm,
        scratch_shapes=list(scratch),
        compiler_params=pltpu.CompilerParams(vmem_limit_bytes=60 * 1024 * 1024),
        cost_estimate=pl.CostEstimate(flops=flops, bytes_accessed=touched, transcendentals=0),
    )(*args)


def cdf_of(value):
    return 0.5 * (1.0 + lax.erf(value * 0.7071067811865476))


def density_of(value):
    return jnp.exp(-0.5 * value * value) * 0.3989422804014327


def dot(a, b):
    return jnp.dot(a, b, preferred_element_type=F32)


def out_terms(factor, out_grad, pre, term, deriv, turned):
    v = pre[...].astype(F32)
    act = (v * cdf_of(v)).astype(BF)
    turned[...] = out_grad[...].T
    width = turned.shape[0] // N
    for k in range(N):
        part = slice(k * width, (k + 1) * width)
        term[part, :] = (dot(turned[part, :], act) * factor).astype(BF)
    rows = pre.shape[0] // N
    i = lax.axis_index(IN)
    u = pre[pl.ds(pl.multiple_of(i * rows, rows), rows), :].astype(F32)
    deriv[...] = cdf_of(u) + u * density_of(u)


def note(flops, *made):
    def body(*refs):
        refs[-1][0, 0] = 0

    return pl.pallas_call(
        body,
        out_shape=sds((1, 1), jnp.int32),
        in_specs=[pl.BlockSpec(memory_space=pl.ANY)] * len(made),
        out_specs=pl.BlockSpec(memory_space=pltpu.SMEM),
        compiler_params=pltpu.CompilerParams(vmem_limit_bytes=60 * 1024 * 1024),
        cost_estimate=pl.CostEstimate(flops=flops, bytes_accessed=0, transcendentals=0),
    )(*made)


def weight_grad(factor, recv, x0, x1, x2, x3, x4, z1, z2, z3, step, step2, step3, out):
    y = lax.axis_index("batch")
    s = 1 - 2 * lax.axis_index("core")
    rows = x0.shape[0] // N
    total = jnp.zeros((out.shape[1], out.shape[0]), F32)
    for k, ref in ((0, x0), (-1, x1), (-2, x2), (-3, x3), (4, x4), (1, z1), (2, z2), (3, z3)):
        at = pl.multiple_of(((y + s * k + N) % N) * rows, rows)
        block = jnp.concatenate([recv[i, pl.ds(at, rows), :] for i in range(N)], 0)
        total = total + dot(block.T, ref[...])
    out[...] = (total * factor).T.astype(BF)


def per_device(inputs, out_grad, pre_act, w_in, w_out):
    tok, d_in = inputs.shape
    hid = pre_act.shape[1]
    factor = 1.0 / math.sqrt(tok * N)
    piece, wide, rows = d_in // N, hid // N, tok // N
    core = lax.axis_index("core")
    scope = jax.named_scope
    fence = lax.optimization_barrier

    def away(a, step, name):
        with scope(name):
            pairs = [(b, (b + step) % N) for b in range(N)]
            pairs += [(N + b, N + (b - step) % N) for b in range(N)]
            return lax.ppermute(a, ("core", "batch"), pairs)

    def swap(a, name):
        with scope(name):
            return lax.ppermute(a, "core", SWAP)

    def spread(a, axis, name):
        with scope(name):
            return lax.all_to_all(a, axis, 0, 0, tiled=True)

    with scope("partial"):
        part = lax.dot_general(out_grad, w_out, (((1,), (1,)), ((), ())), preferred_element_type=F32)
        part = part.astype(BF).reshape(N, rows, hid)
    got = spread(part, IN, "hidden_reduce")
    x1 = away(inputs, 1, "x1")
    with scope("out_terms"):
        w_out_term, deriv = call(
            functools.partial(out_terms, factor),
            [sds((d_in, hid)), sds((rows, hid), F32)],
            out_grad,
            pre_act,
            scratch=[pltpu.VMEM((d_in, tok), BF)],
        )
    with scope("w_out_sum"):
        w_out_grad = lax.psum_scatter(w_out_term, "batch", scatter_dimension=0, tiled=True).T

    with scope("hidden_grad"):
        total = jnp.sum(got.astype(F32), axis=0)
        mine = (total * deriv).astype(BF)
    mine, w_out_term = fence((mine, w_out_term))
    with scope("hidden_copy"):
        copies = jnp.broadcast_to(mine, (N, rows, hid))
    pg = spread(copies, IN, "hidden_spread").reshape(tok, hid)
    with scope("hidden_blocks"):
        blocks = mine.reshape(rows, N, wide).swapaxes(0, 1)
    x2 = away(x1, 1, "x2")
    z1 = swap(x1, "z1")
    with scope("step"):
        step = note(3000000000, z1)
    pg, blocks, step = fence((pg, blocks, step))
    across = spread(blocks, "batch", "batch_spread")

    with scope("input_term"):
        term = lax.dot_general(w_in, pg, (((1,), (1,)), ((), ())), preferred_element_type=F32)
        term = term.astype(BF).reshape(4, 2, piece, tok)
    with scope("send_half"):
        far_half = lax.dynamic_index_in_dim(term, 1 - core, 1, False)
    got_half = swap(far_half, "half_swap")
    far_half, x2 = fence((far_half, x2))
    x3 = away(x2, 1, "x3")
    z2 = swap(x2, "z2")
    with scope("keep_half"):
        near = lax.dynamic_index_in_dim(term, core, 1, False)
        kept = (near.astype(F32) + got_half.astype(F32)).astype(BF)
    with scope("step2"):
        step2 = note(3000000000, across)
    across, step2 = fence((across, step2))
    with scope("across_copy"):
        copies = jnp.broadcast_to(across, (N, N, rows, wide))
    recv = spread(copies, IN, "across_spread").reshape(N, tok, wide)
    x4 = away(x3, 1, "x4")
    z3 = swap(x3, "z3")
    with scope("step3"):
        step3 = note(6000000000, x3)
    recv, kept, step3 = fence((recv, kept, step3))
    quad = spread(kept, "zhi", "zhi_spread")
    with scope("weight_grad"):
        w_in_grad = call(
            functools.partial(weight_grad, factor),
            sds((d_in, wide)),
            recv, inputs, x1, x2, x3, x4, z1, z2, z3, step, step2, step3,
            hold=3,
        )
    quad, w_in_grad = fence((quad, w_in_grad))
    with scope("sum_four"):
        input_grad = jnp.sum(quad.astype(F32), axis=0).astype(BF).T
    return (input_grad, w_in_grad, w_out_grad)


def solution(mesh):
    fine = Mesh(mesh.devices.reshape(4, 2, 4, 2, 8), ("x", "zlo", "zhi", "core", "batch"))
    return jax.shard_map(
        per_device,
        mesh=fine,
        in_specs=(P("batch", IN), P("batch", IN), P("batch", OUT), P(IN, OUT), P(OUT, IN)),
        out_specs=(P("batch", IN + OUT), P(IN, OUT + ("batch",)), P(OUT, IN + ("batch",))),
        check_vma=False,
    )
```

```python
import functools
import math

import jax
import jax.numpy as jnp
from jax import lax
from jax.experimental import pallas as pl
from jax.experimental.pallas import tpu as pltpu
from jax.sharding import Mesh, PartitionSpec as P

BF = jnp.bfloat16
F32 = jnp.float32
IN = ("x", "zlo")
OUT = ("zhi", "core")
SWAP = [(0, 1), (1, 0)]
N = 8
RING = [(b, (b + 1) % N) for b in range(N)] + [(N + b, N + (b - 1) % N) for b in range(N)]


def sds(shape, dtype=BF):
    return jax.ShapeDtypeStruct(shape, dtype)


def call(body, outs, *args, scratch=(), flops=0, touched=0, hold=0):
    vm = pl.BlockSpec(memory_space=pltpu.VMEM)
    many = isinstance(outs, (list, tuple))
    return pl.pallas_call(
        body,
        out_shape=outs,
        in_specs=[vm] * (len(args) - hold) + [pl.BlockSpec(memory_space=pl.ANY)] * hold,
        out_specs=[vm] * len(outs) if many else vm,
        scratch_shapes=list(scratch),
        compiler_params=pltpu.CompilerParams(vmem_limit_bytes=60 * 1024 * 1024),
        cost_estimate=pl.CostEstimate(flops=flops, bytes_accessed=touched, transcendentals=0),
    )(*args)


def cdf_of(value):
    return 0.5 * (1.0 + lax.erf(value * 0.7071067811865476))


def density_of(value):
    return jnp.exp(-0.5 * value * value) * 0.3989422804014327


def dot(a, b):
    return jnp.dot(a, b, preferred_element_type=F32)


def ring_sign():
    return 1 - 2 * lax.axis_index("core")


def out_terms(factor, out_grad, pre, term, deriv, turned):
    v = pre[...].astype(F32)
    act = (v * cdf_of(v)).astype(BF)
    turned[...] = out_grad[...].T
    width = turned.shape[0] // N
    for k in range(N):
        part = slice(k * width, (k + 1) * width)
        term[part, :] = (dot(turned[part, :], act) * factor).astype(BF)
    i = lax.axis_index(IN)
    wide = pre.shape[1] // N
    u = pre[:, pl.ds(pl.multiple_of(i * wide, wide), wide)].astype(F32)
    deriv[...] = (cdf_of(u) + u * density_of(u)).T


def note(flops, *made):
    def body(*refs):
        refs[-1][0, 0] = 0

    return pl.pallas_call(
        body,
        out_shape=sds((1, 1), jnp.int32),
        in_specs=[pl.BlockSpec(memory_space=pl.ANY)] * len(made),
        out_specs=pl.BlockSpec(memory_space=pltpu.SMEM),
        compiler_params=pltpu.CompilerParams(vmem_limit_bytes=60 * 1024 * 1024),
        cost_estimate=pl.CostEstimate(flops=flops, bytes_accessed=0, transcendentals=0),
    )(*made)


def weight_part(at, last, own, other, *refs):
    y = lax.axis_index("batch")
    s = 1 - 2 * lax.axis_index("core")
    first = lax.axis_index("zlo") == 0
    out = refs[-1]
    total = refs[len(at)][...] if last else jnp.zeros(out.shape, F32)
    for k, ref in zip(at, refs):
        b = (y + s * k + N) % N
        a, c = own[b], other[b]
        block = jnp.concatenate([jnp.where(first, a, c), jnp.where(first, c, a)], 1)
        total = total + dot(block, ref[...])
    out[...] = (total * last).T.astype(BF) if last else total


def per_device(inputs, out_grad, pre_act, w_in, w_out):
    tok, d_in = inputs.shape
    hid = pre_act.shape[1]
    factor = 1.0 / math.sqrt(tok * N)
    piece, wide = d_in // N, hid // N
    core = lax.axis_index("core")
    scope = jax.named_scope
    fence = lax.optimization_barrier

    def away(a, step, name):
        with scope(name):
            pairs = [(b, (b + step) % N) for b in range(N)]
            pairs += [(N + b, N + (b - step) % N) for b in range(N)]
            return lax.ppermute(a, ("core", "batch"), pairs)

    def swap(a, name):
        with scope(name):
            return lax.ppermute(a, "core", SWAP)

    def spread(a, axis, name):
        with scope(name):
            return lax.all_to_all(a, axis, 0, 0, tiled=True)

    with scope("partial"):
        part = lax.dot_general(w_out, out_grad, (((1,), (1,)), ((), ())), preferred_element_type=F32)
        part = part.astype(BF).reshape(N, wide, tok)
    got = spread(part, IN, "hidden_reduce")
    x1 = away(inputs, 1, "x1")
    with scope("out_terms"):
        w_out_term, deriv = call(
            functools.partial(out_terms, factor),
            [sds((d_in, hid)), sds((wide, tok), F32)],
            out_grad,
            pre_act,
            scratch=[pltpu.VMEM((d_in, tok), BF)],
        )
    with scope("w_out_sum"):
        w_out_grad = lax.psum_scatter(w_out_term, "batch", scatter_dimension=0, tiled=True).T

    with scope("hidden_grad"):
        total = jnp.sum(got.astype(F32), axis=0)
        mine = (total * deriv).astype(BF)
    mine, w_out_term = fence((mine, w_out_term))
    with scope("hidden_copy"):
        mine = jnp.broadcast_to(mine, (N, wide, tok))
    pg = spread(mine, IN, "hidden_spread")
    x2 = away(x1, 1, "x2")
    z1 = swap(x1, "z1")
    with scope("step"):
        step = note(3000000000, z1)
    pg, step = fence((pg, step))
    with scope("own_tokens"):
        cols = lax.dynamic_slice_in_dim(pg, lax.axis_index("zlo") * (tok // 2), tok // 2, 2)
    cols = spread(cols, "batch", "batch_spread")
    with scope("input_term"):
        term = lax.dot_general(
            w_in, pg.reshape(hid, tok), (((1,), (0,)), ((), ())), preferred_element_type=F32
        ).astype(BF).reshape(4, 2, piece, tok)
    with scope("send_half"):
        far_half = lax.dynamic_index_in_dim(term, 1 - core, 1, False)
    got_half = swap(far_half, "half_swap")
    far_half, x2 = fence((far_half, x2))
    x3, x4 = away(x2, 1, "x3"), away(x2, 2, "x4")
    with scope("keep_half"):
        near = lax.dynamic_index_in_dim(term, core, 1, False)
        kept = (near.astype(F32) + got_half.astype(F32)).astype(BF)
    with scope("step2"):
        step2 = note(3000000000, cols)
    cols, kept, step2 = fence((cols, kept, step2))
    with scope("zlo_swap"):
        more = lax.ppermute(cols, "zlo", SWAP)
    quad = spread(kept, "zhi", "zhi_spread")
    z2 = swap(x2, "z2")
    more, x3 = fence((more, x3))
    z3 = swap(x3, "z3")
    with scope("weight_grad"):
        early = call(
            functools.partial(weight_part, (0, -1, -2, 1, 2), 0.0),
            sds((wide, d_in), F32),
            cols, more, inputs, x1, x2, z1, z2, step, step2,
            flops=6000000000,
            hold=2,
        )
        w_in_grad = call(
            functools.partial(weight_part, (-3, 4, 3), factor),
            sds((d_in, wide)),
            cols, more, x3, x4, z3, early,
            hold=0,
        )
    quad, w_in_grad = fence((quad, w_in_grad))
    with scope("sum_four"):
        input_grad = jnp.sum(quad.astype(F32), axis=0).astype(BF).T
    return (input_grad, w_in_grad, w_out_grad)


def solution(mesh):
    fine = Mesh(mesh.devices.reshape(4, 2, 4, 2, 8), ("x", "zlo", "zhi", "core", "batch"))
    return jax.shard_map(
        per_device,
        mesh=fine,
        in_specs=(P("batch", IN), P("batch", IN), P("batch", OUT), P(IN, OUT), P(OUT, IN)),
        out_specs=(P("batch", IN + OUT), P(IN, OUT + ("batch",)), P(OUT, IN + ("batch",))),
        check_vma=False,
    )
```

```python
import functools
import math

import jax
import jax.numpy as jnp
from jax import lax
from jax.experimental import pallas as pl
from jax.experimental.pallas import tpu as pltpu
from jax.sharding import Mesh, PartitionSpec as P

BF = jnp.bfloat16
F32 = jnp.float32
IN = ("x", "zlo")
OUT = ("zhi", "core")
SWAP = [(0, 1), (1, 0)]
N = 8
RING = [(b, (b + 1) % N) for b in range(N)] + [(N + b, N + (b - 1) % N) for b in range(N)]


def sds(shape, dtype=BF):
    return jax.ShapeDtypeStruct(shape, dtype)


def call(body, outs, *args, scratch=(), flops=0, touched=0, hold=0, room=60):
    vm = pl.BlockSpec(memory_space=pltpu.VMEM)
    many = isinstance(outs, (list, tuple))
    return pl.pallas_call(
        body,
        out_shape=outs,
        in_specs=[vm] * (len(args) - hold) + [pl.BlockSpec(memory_space=pl.ANY)] * hold,
        out_specs=[vm] * len(outs) if many else vm,
        scratch_shapes=list(scratch),
        compiler_params=pltpu.CompilerParams(vmem_limit_bytes=room * 1024 * 1024),
        cost_estimate=pl.CostEstimate(flops=flops, bytes_accessed=touched, transcendentals=0),
    )(*args)


def cdf_of(value):
    return 0.5 * (1.0 + lax.erf(value * 0.7071067811865476))


def density_of(value):
    return jnp.exp(-0.5 * value * value) * 0.3989422804014327


def dot(a, b):
    return jnp.dot(a, b, preferred_element_type=F32)


def ring_sign():
    return 1 - 2 * lax.axis_index("core")


def out_terms(factor, out_grad, pre, term, deriv, turned):
    v = pre[...].astype(F32)
    act = (v * cdf_of(v)).astype(BF)
    turned[...] = out_grad[...].T
    width = turned.shape[0] // N
    for k in range(N):
        part = slice(k * width, (k + 1) * width)
        term[part, :] = (dot(turned[part, :], act) * factor).astype(BF)
    i = lax.axis_index(IN)
    wide = pre.shape[1] // N
    u = pre[:, pl.ds(pl.multiple_of(i * wide, wide), wide)].astype(F32)
    deriv[...] = (cdf_of(u) + u * density_of(u)).T


def note(flops, *made):
    def body(*refs):
        refs[-1][0, 0] = 0

    return pl.pallas_call(
        body,
        out_shape=sds((1, 1), jnp.int32),
        in_specs=[pl.BlockSpec(memory_space=pl.ANY)] * len(made),
        out_specs=pl.BlockSpec(memory_space=pltpu.SMEM),
        compiler_params=pltpu.CompilerParams(vmem_limit_bytes=60 * 1024 * 1024),
        cost_estimate=pl.CostEstimate(flops=flops, bytes_accessed=0, transcendentals=0),
    )(*made)


def weight_part(at, last, own, other, *refs):
    y = lax.axis_index("batch")
    s = 1 - 2 * lax.axis_index("core")
    first = lax.axis_index("zlo") == 0
    out = refs[-1]
    total = refs[len(at)][...].astype(F32) if last else jnp.zeros(out.shape, F32)
    for k, ref in zip(at, refs):
        b = (y + s * k + N) % N
        a, c = own[b], other[b]
        block = jnp.concatenate([jnp.where(first, a, c), jnp.where(first, c, a)], 1)
        total = total + dot(block, ref[...])
    out[...] = (total * last).T.astype(BF) if last else total.astype(BF)


def per_device(inputs, out_grad, pre_act, w_in, w_out):
    tok, d_in = inputs.shape
    hid = pre_act.shape[1]
    factor = 1.0 / math.sqrt(tok * N)
    piece, wide = d_in // N, hid // N
    core = lax.axis_index("core")
    scope = jax.named_scope
    fence = lax.optimization_barrier

    def away(a, step, name):
        with scope(name):
            pairs = [(b, (b + step) % N) for b in range(N)]
            pairs += [(N + b, N + (b - step) % N) for b in range(N)]
            return lax.ppermute(a, ("core", "batch"), pairs)

    def swap(a, name):
        with scope(name):
            return lax.ppermute(a, "core", SWAP)

    def spread(a, axis, name):
        with scope(name):
            return lax.all_to_all(a, axis, 0, 0, tiled=True)

    with scope("partial"):
        part = lax.dot_general(w_out, out_grad, (((1,), (1,)), ((), ())), preferred_element_type=F32)
        part = part.astype(BF).reshape(N, wide, tok)
    got = spread(part, IN, "hidden_reduce")
    x1 = away(inputs, 1, "x1")
    with scope("out_terms"):
        w_out_term, deriv = call(
            functools.partial(out_terms, factor),
            [sds((d_in, hid)), sds((wide, tok), F32)],
            out_grad,
            pre_act,
            scratch=[pltpu.VMEM((d_in, tok), BF)],
        )
    with scope("w_out_sum"):
        w_out_grad = lax.psum_scatter(w_out_term, "batch", scatter_dimension=0, tiled=True).T

    with scope("hidden_grad"):
        total = jnp.sum(got.astype(F32), axis=0)
        mine = (total * deriv).astype(BF)
    mine, w_out_term = fence((mine, w_out_term))
    with scope("hidden_copy"):
        mine = jnp.broadcast_to(mine, (N, wide, tok))
    pg = spread(mine, IN, "hidden_spread")
    x2 = away(x1, 1, "x2")
    z1 = swap(x1, "z1")
    with scope("step"):
        step = note(3000000000, z1)
    pg, step = fence((pg, step))
    with scope("own_tokens"):
        cols = lax.dynamic_slice_in_dim(pg, lax.axis_index("zlo") * (tok // 2), tok // 2, 2)
    cols = spread(cols, "batch", "batch_spread")
    with scope("input_term"):
        term = lax.dot_general(
            w_in, pg.reshape(hid, tok), (((1,), (0,)), ((), ())), preferred_element_type=F32
        ).astype(BF).reshape(4, 2, piece, tok)
    with scope("send_half"):
        far_half = lax.dynamic_index_in_dim(term, 1 - core, 1, False)
    got_half = swap(far_half, "half_swap")
    far_half, x2 = fence((far_half, x2))
    x3, x4 = away(x2, 1, "x3"), away(x2, 2, "x4")
    with scope("keep_half"):
        near = lax.dynamic_index_in_dim(term, core, 1, False)
        kept = (near.astype(F32) + got_half.astype(F32)).astype(BF)
    with scope("step2"):
        step2 = note(3000000000, cols)
    cols, kept, step2 = fence((cols, kept, step2))
    with scope("zlo_swap"):
        more = lax.ppermute(cols, "zlo", SWAP)
    quad = spread(kept, "zhi", "zhi_spread")
    z2 = swap(x2, "z2")
    more, x3 = fence((more, x3))
    z3 = swap(x3, "z3")
    with scope("weight_grad"):
        early = call(
            functools.partial(weight_part, (0, -1, -2, 1, 2), 0.0),
            sds((wide, d_in)),
            cols, more, inputs, x1, x2, z1, z2, step, step2,
            flops=6000000000,
            hold=2,
            room=62,
        )
        w_in_grad = call(
            functools.partial(weight_part, (-3, 4, 3), factor),
            sds((d_in, wide)),
            cols, more, x3, x4, z3, early,
            room=62,
        )
    quad, w_in_grad = fence((quad, w_in_grad))
    with scope("sum_four"):
        input_grad = jnp.sum(quad.astype(F32), axis=0).astype(BF).T
    return (input_grad, w_in_grad, w_out_grad)


def solution(mesh):
    fine = Mesh(mesh.devices.reshape(4, 2, 4, 2, 8), ("x", "zlo", "zhi", "core", "batch"))
    return jax.shard_map(
        per_device,
        mesh=fine,
        in_specs=(P("batch", IN), P("batch", IN), P("batch", OUT), P(IN, OUT), P(OUT, IN)),
        out_specs=(P("batch", IN + OUT), P(IN, OUT + ("batch",)), P(OUT, IN + ("batch",))),
        check_vma=False,
    )
```

```python
import functools
import math

import jax
import jax.numpy as jnp
from jax import lax
from jax.experimental import pallas as pl
from jax.experimental.pallas import tpu as pltpu
from jax.sharding import Mesh, PartitionSpec as P

BF = jnp.bfloat16
F32 = jnp.float32
IN = ("x", "zlo")
OUT = ("zhi", "core")
SWAP = [(0, 1), (1, 0)]
N = 8
RING = [(b, (b + 1) % N) for b in range(N)] + [(N + b, N + (b - 1) % N) for b in range(N)]


def sds(shape, dtype=BF):
    return jax.ShapeDtypeStruct(shape, dtype)


def call(body, outs, *args, scratch=(), flops=0, touched=0, hold=0, room=60):
    vm = pl.BlockSpec(memory_space=pltpu.VMEM)
    many = isinstance(outs, (list, tuple))
    return pl.pallas_call(
        body,
        out_shape=outs,
        in_specs=[vm] * (len(args) - hold) + [pl.BlockSpec(memory_space=pl.ANY)] * hold,
        out_specs=[vm] * len(outs) if many else vm,
        scratch_shapes=list(scratch),
        compiler_params=pltpu.CompilerParams(vmem_limit_bytes=room * 1024 * 1024),
        cost_estimate=pl.CostEstimate(flops=flops, bytes_accessed=touched, transcendentals=0),
    )(*args)


def cdf_of(value):
    return 0.5 * (1.0 + lax.erf(value * 0.7071067811865476))


def density_of(value):
    return jnp.exp(-0.5 * value * value) * 0.3989422804014327


def dot(a, b):
    return jnp.dot(a, b, preferred_element_type=F32)


def ring_sign():
    return 1 - 2 * lax.axis_index("core")


def out_terms(factor, out_grad, pre, term, deriv, turned):
    v = pre[...].astype(F32)
    act = (v * cdf_of(v)).astype(BF)
    turned[...] = out_grad[...].T
    width = turned.shape[0] // N
    for k in range(N):
        part = slice(k * width, (k + 1) * width)
        term[part, :] = (dot(turned[part, :], act) * factor).astype(BF)
    i = lax.axis_index(IN)
    wide = pre.shape[1] // N
    u = pre[:, pl.ds(pl.multiple_of(i * wide, wide), wide)].astype(F32)
    deriv[...] = (cdf_of(u) + u * density_of(u)).T


def note(flops, *made):
    def body(*refs):
        refs[-1][0, 0] = 0

    return pl.pallas_call(
        body,
        out_shape=sds((1, 1), jnp.int32),
        in_specs=[pl.BlockSpec(memory_space=pl.ANY)] * len(made),
        out_specs=pl.BlockSpec(memory_space=pltpu.SMEM),
        compiler_params=pltpu.CompilerParams(vmem_limit_bytes=16 * 1024 * 1024),
        cost_estimate=pl.CostEstimate(flops=flops, bytes_accessed=0, transcendentals=0),
    )(*made)


def weight_part(at, last, own, other, *refs):
    y = lax.axis_index("batch")
    s = 1 - 2 * lax.axis_index("core")
    first = lax.axis_index("zlo") == 0
    out = refs[-1]
    total = refs[len(at)][...].astype(F32) if last else jnp.zeros(out.shape, F32)
    for k, ref in zip(at, refs):
        b = (y + s * k + N) % N
        a, c = own[b], other[b]
        block = jnp.concatenate([jnp.where(first, a, c), jnp.where(first, c, a)], 1)
        total = total + dot(block, ref[...])
    out[...] = (total * last).T.astype(BF) if last else total.astype(BF)


def per_device(inputs, out_grad, pre_act, w_in, w_out):
    tok, d_in = inputs.shape
    hid = pre_act.shape[1]
    factor = 1.0 / math.sqrt(tok * N)
    piece, wide = d_in // N, hid // N
    core = lax.axis_index("core")
    scope = jax.named_scope
    fence = lax.optimization_barrier

    def away(a, step, name):
        with scope(name):
            pairs = [(b, (b + step) % N) for b in range(N)]
            pairs += [(N + b, N + (b - step) % N) for b in range(N)]
            return lax.ppermute(a, ("core", "batch"), pairs)

    def swap(a, name):
        with scope(name):
            return lax.ppermute(a, "core", SWAP)

    def spread(a, axis, name):
        with scope(name):
            return lax.all_to_all(a, axis, 0, 0, tiled=True)

    with scope("partial"):
        part = lax.dot_general(w_out, out_grad, (((1,), (1,)), ((), ())), preferred_element_type=F32)
        part = part.astype(BF).reshape(N, wide, tok)
    got = spread(part, IN, "hidden_reduce")
    x1 = away(inputs, 1, "x1")
    with scope("out_terms"):
        w_out_term, deriv = call(
            functools.partial(out_terms, factor),
            [sds((d_in, hid)), sds((wide, tok), F32)],
            out_grad,
            pre_act,
            scratch=[pltpu.VMEM((d_in, tok), BF)],
        )
    with scope("w_out_sum"):
        w_out_grad = lax.psum_scatter(w_out_term, "batch", scatter_dimension=0, tiled=True).T

    with scope("hidden_grad"):
        total = jnp.sum(got.astype(F32), axis=0)
        mine = (total * deriv).astype(BF)
    mine, w_out_term = fence((mine, w_out_term))
    with scope("hidden_copy"):
        mine = jnp.broadcast_to(mine, (N, wide, tok))
    pg = spread(mine, IN, "hidden_spread")
    x2 = away(x1, 1, "x2")
    z1 = swap(x1, "z1")
    with scope("step"):
        step = note(3000000000, z1)
    pg, step = fence((pg, step))
    with scope("own_tokens"):
        cols = lax.dynamic_slice_in_dim(pg, lax.axis_index("zlo") * (tok // 2), tok // 2, 2)
    cols = spread(cols, "batch", "batch_spread")
    with scope("input_term"):
        term = lax.dot_general(
            w_in, pg.reshape(hid, tok), (((1,), (0,)), ((), ())), preferred_element_type=F32
        ).astype(BF).reshape(4, 2, piece, tok)
    with scope("send_half"):
        far_half = lax.dynamic_index_in_dim(term, 1 - core, 1, False)
    got_half = swap(far_half, "half_swap")
    far_half, x2 = fence((far_half, x2))
    x3, x4 = away(x2, 1, "x3"), away(x2, 2, "x4")
    with scope("keep_half"):
        near = lax.dynamic_index_in_dim(term, core, 1, False)
        kept = (near.astype(F32) + got_half.astype(F32)).astype(BF)
    with scope("step2"):
        step2 = note(3000000000, cols)
    cols, kept, step2 = fence((cols, kept, step2))
    with scope("zlo_swap"):
        more = lax.ppermute(cols, "zlo", SWAP)
    quad = spread(kept, "zhi", "zhi_spread")
    z2 = swap(x2, "z2")
    more, x3 = fence((more, x3))
    z3 = swap(x3, "z3")
    with scope("weight_grad"):
        early = call(
            functools.partial(weight_part, (0, -1, -2, 1, 2), 0.0),
            sds((wide, d_in)),
            cols, more, inputs, x1, x2, z1, z2, step, step2,
            flops=6000000000,
            hold=2,
            room=62,
        )
        w_in_grad = call(
            functools.partial(weight_part, (-3, 4, 3), factor),
            sds((d_in, wide)),
            cols, more, x3, x4, z3, early,
            room=62,
        )
    quad, w_in_grad = fence((quad, w_in_grad))
    with scope("sum_four"):
        input_grad = jnp.sum(quad.astype(F32), axis=0).astype(BF).T
    return (input_grad, w_in_grad, w_out_grad)


def solution(mesh):
    fine = Mesh(mesh.devices.reshape(4, 2, 4, 2, 8), ("x", "zlo", "zhi", "core", "batch"))
    return jax.shard_map(
        per_device,
        mesh=fine,
        in_specs=(P("batch", IN), P("batch", IN), P("batch", OUT), P(IN, OUT), P(OUT, IN)),
        out_specs=(P("batch", IN + OUT), P(IN, OUT + ("batch",)), P(OUT, IN + ("batch",))),
        check_vma=False,
    )
```
